32 devices in a mesh: groups: 2 (over x), tensor: 16 (over z, y, core).
Axes of the slice: x: 2, y: 2, z: 4, core: 2. Of those that a mesh axis runs over, the one named last changes fastest.
Arguments:
- attention_output_rows: bfloat16 [512, 8192], P(('groups', 'tensor')), parts along dimension 0, may hold values from -6 to 6
- output_projection_weight: bfloat16 [8192, 8192], P(None, 'tensor'), may hold values from -0.0625 to 0.0625
- adapter_down_matrices: bfloat16 [256, 8192, 64], P(None, 'tensor'), may hold values from -0.0625 to 0.0625
- adapter_up_matrices: bfloat16 [256, 64, 8192], P(None, None, 'tensor'), may hold values from -0.75 to 0.75
- picks: int32 [512, 2], P('groups'), parts along dimension 0, may hold values from 0 to 255, all different within a row; in each aligned block of 256 rows (0 to 255, 256 to 511, ...) at most 8 rows name the same one
- gates: float32 [512, 2], P('groups'), parts along dimension 0, may hold values from 0.2 to 1
- adapter_storage_index: int32 [256], replicated, may hold values from 0 to 255, each once
Outputs:
- mixed: bfloat16 [512, 8192], P('groups', 'tensor'), parts along dimension 0
The draws below stay inside these ranges and needn't reach their ends.
There are 2 independent parts, one for each index of `groups`. The reference program is written for one: setup_inputs(seed, part) draws one part's arguments, and reference() takes and returns one part's arrays. A program takes and returns all parts, laid end to end along the dimension named above; an argument that names none is the same for every part. Nothing has to cross between parts.
Inputs may be any that keep to these rules, and one draw needn't show every extreme that they name: `picks`: each token names two different adapters; over the 256 tokens of a replica no adapter is named more than 8 times, a bound that some block reaches. A permutation: the matrices of adapter e lie at index adapter_storage_index[e] of adapter_down_matrices and adapter_up_matrices.
All inputs are finite; a program needn't handle non-finite values.
Results may differ from the reference program's by a relative error of at most 0.0038.
Values may be sent and summed in bfloat16 or wider, within the bound.
A program may use at most 128 MiB of HBM per device.

```python
import math
import jax
import jax.numpy as jnp
import numpy as np
from jax import lax

MODEL_WIDTH = 8192
ADAPTER_TOTAL = 256
ADAPTER_RANK = 64
TOKENS = 256
PEAK_TOKENS = 8


def levels(key, extent, pieces, least, high):
    loudness, own = 1.0, jax.random.fold_in(key, 6)
    for dim, blocks in pieces:
        draws = jnp.exp(jax.random.uniform(jax.random.fold_in(own, dim), (blocks,), jnp.float32, least / len(pieces), high / len(pieces)))
        loudness = loudness * jnp.repeat(draws, extent[dim] // blocks).reshape([-1 if axis == dim else 1 for axis in range(len(extent))])
    return loudness


def routed_block(key, own, number, rows, amount, top, limit, slope):
    sequence = jax.random.permutation(key, amount)
    packed, usual = portions_of(amount, rows * top, limit, slope, True), portions_of(amount, rows * top, limit, slope, False)
    places = jnp.arange(amount)

    def named(tallies, rotation):
        used = int((tallies > 0).sum())
        fixed = max(1, used // 4)
        moved = fixed + (places - fixed + rotation * (used - fixed)) % max(1, amount - fixed)
        return jnp.zeros((amount,), jnp.int32).at[sequence[jnp.where(places < fixed, places, moved)]].set(jnp.asarray(tallies, jnp.int32))

    tallies = jnp.where(number % 4 == 0, named(packed, number // 4), named(usual, number - number // 4 - 1))
    mixed = jax.random.permutation(jax.random.fold_in(own, 3), amount)
    giver, sink = mixed[0:amount // 2 * 2:2], mixed[1:amount // 2 * 2:2]
    slack = jnp.minimum(tallies[giver] - 1, limit - tallies[sink]) // 2
    slack = jnp.where((giver == sequence[0]) | (sink == sequence[0]) | (tallies[sink] == 0), 0, jnp.maximum(slack, 0))
    moved = jax.random.randint(jax.random.fold_in(own, 4), (amount // 2,), 0, 1 << 20) % (slack + 1)
    tallies = tallies.at[giver].add(-moved).at[sink].add(moved)
    items = jnp.searchsorted(jnp.cumsum(tallies), jnp.arange(rows * top), side="right").astype(jnp.int32)
    table = items.reshape(top, rows).T
    table = table[jax.random.permutation(jax.random.fold_in(own, 1), rows)]
    rotation = jax.random.randint(jax.random.fold_in(own, 2), (rows, 1), 0, top)
    return jnp.take_along_axis(table, (jnp.arange(top)[None, :] + rotation) % top, axis=1)


def portions_of(number_of, total, bound, slope, full):
    loads = [(1 << 20) // math.isqrt(grade ** slope) + 1 for grade in range(1, number_of + 1)]
    largest = bound if full else min(bound, max(-(-total // number_of), total * loads[0] // sum(loads)))
    least = 1 if total - largest >= number_of - 1 else 0
    holding, surplus = [largest] + [least] * (number_of - 1), total - largest - least * (number_of - 1)
    while surplus > 0:
        candidates = [i for i in range(1, number_of) if holding[i] < largest] or [i for i in range(1, number_of) if holding[i] < bound]
        whole, remaining = sum([loads[i] for i in candidates]), surplus
        for i in candidates:
            addition = min(bound - holding[i], max(1, remaining * loads[i] // whole), surplus)
            holding[i] = holding[i] + addition
            surplus = surplus - addition
    return np.array(holding)


def centred(key, dims, spread, limit, cuts=(), kind=jnp.bfloat16):
    factor_of = levels(key, dims, cuts, -0.22, 0.18) if cuts else 1.0
    drawn = jax.random.normal(key, dims, jnp.float32) * spread * factor_of
    return jnp.minimum(jnp.maximum(drawn, -limit), limit).astype(kind)


def setup_inputs(seed: int = 0, part: int = 0) -> dict:
    streams_of = jax.random.split(jax.random.key(seed), 8)
    own_keys = jax.random.split(jax.random.fold_in(streams_of[7], part), 8)
    attention_output_rows = centred(own_keys[0], (TOKENS, MODEL_WIDTH), 1.0, 6.0, ((0, 16),))
    output_projection_weight = centred(streams_of[1], (MODEL_WIDTH, MODEL_WIDTH), MODEL_WIDTH ** -0.5, 0.0625, ((1, 16),))
    adapter_down_matrices = centred(streams_of[2], (ADAPTER_TOTAL, MODEL_WIDTH, ADAPTER_RANK), MODEL_WIDTH ** -0.5, 0.0625, ((1, 16),))
    adapter_up_matrices = centred(streams_of[3], (ADAPTER_TOTAL, ADAPTER_RANK, MODEL_WIDTH), ADAPTER_RANK ** -0.5, 0.75, ((2, 16),))
    picks_keys = jax.random.split(jax.random.fold_in(own_keys[4], 1), TOKENS // TOKENS)
    picks_turns = jax.random.permutation(jax.random.fold_in(own_keys[4], 3), TOKENS // TOKENS)
    picks = jax.vmap(lambda own, number: routed_block(jax.random.fold_in(own_keys[4], 2), own, number, TOKENS, ADAPTER_TOTAL, 2, PEAK_TOKENS, 2))(picks_keys, picks_turns).reshape((TOKENS, 2))
    gates = jnp.clip(jax.random.uniform(own_keys[5], (TOKENS, 2), jnp.float32, 0.2, 1.0), 0.2, 1.0)
    adapter_storage_index = jax.random.permutation(streams_of[6], ADAPTER_TOTAL).astype(jnp.int32)
    return dict(attention_output_rows=attention_output_rows, output_projection_weight=output_projection_weight, adapter_down_matrices=adapter_down_matrices, adapter_up_matrices=adapter_up_matrices, picks=picks, gates=gates, adapter_storage_index=adapter_storage_index)


def routing(picks, gates, adapter_storage_index, storage_count, most):
    chosen = picks.reshape(-1)
    slot_of = jnp.take(adapter_storage_index, chosen)
    onehot = (slot_of[:, None] == jnp.arange(storage_count, dtype=jnp.int32)[None, :]).astype(jnp.int32)
    order_in = jnp.sum((jnp.cumsum(onehot, axis=0) - onehot) * onehot, axis=1).astype(jnp.int32)
    position = slot_of * most + order_in
    token_ids = (jnp.arange(chosen.shape[0], dtype=jnp.int32) // 2).astype(jnp.int32)
    token_of = jnp.zeros((storage_count * most,), jnp.int32).at[position].set(token_ids)
    token_gate_weight = jnp.zeros((storage_count * most,), jnp.float32).at[position].set(gates.reshape(-1))
    live = jnp.zeros((storage_count * most,), jnp.float32).at[position].set(jnp.ones_like(gates.reshape(-1)))
    return token_of, token_gate_weight, live


def shrink_single_adapter(pair):
    rows, matrix = pair
    return jnp.dot(rows, matrix, preferred_element_type=jnp.float32)


def expand_single_adapter(triple):
    vectors, matrix, weights = triple
    return jnp.dot(vectors, matrix, preferred_element_type=jnp.float32) * weights[:, None]


def reference(attention_output_rows, output_projection_weight, adapter_down_matrices, adapter_up_matrices, picks, gates, adapter_storage_index):
    token_of, token_gate_weight, live = routing(picks, gates, adapter_storage_index, ADAPTER_TOTAL, PEAK_TOKENS)
    base = jnp.dot(attention_output_rows, output_projection_weight, preferred_element_type=jnp.float32)
    routed_token_rows = (attention_output_rows[token_of] * live[:, None].astype(attention_output_rows.dtype)).reshape(ADAPTER_TOTAL, PEAK_TOKENS, MODEL_WIDTH)
    reduced_rank_rows = lax.map(shrink_single_adapter, (routed_token_rows, adapter_down_matrices)).astype(jnp.bfloat16)
    expanded_rows = lax.map(expand_single_adapter, (reduced_rank_rows, adapter_up_matrices, token_gate_weight.reshape(ADAPTER_TOTAL, PEAK_TOKENS)))
    total = base.at[token_of].add(expanded_rows.reshape(ADAPTER_TOTAL * PEAK_TOKENS, MODEL_WIDTH))
    return total.astype(jnp.bfloat16)
```

```python
import functools

import jax
import jax.numpy as jnp
from jax import lax
from jax.experimental import pallas as pl
from jax.experimental.pallas import tpu as pltpu
from jax.sharding import PartitionSpec as P

MESH = pl.DeviceIdType.MESH
Z, Y, C = 4, 2, 2
N = Z * Y * C
Q = 4
LOADS = 16


def fused(
    x_ref, w_ref, down_ref, up_ref, picks_ref, gates_ref, index_ref, out_ref,
    gathered, block, w_vm, down_vm, up_vm, product, mixed_rows, partial, pieces, reduced, total,
    load_sem, w_sem, own_sem, a2a_send, a2a_recv, z_send, y_send, c_send, recv,
    rs_send, rs_recv, ag_send, ag_recv,
):
    rows = x_ref.shape[0]
    tokens = rows * N
    feat = block.shape[1]
    kq = gathered.shape[2]
    stored = index_ref.shape[0]
    rank = down_ref.shape[0] // stored
    per = stored // LOADS
    span = per * rank
    me = lax.axis_index("tensor")
    z = me // (Y * C)
    yc = me % (Y * C)
    y = yc // C
    c = yc % C

    def dev(zz, yy, cc):
        return (zz * Y + yy) * C + cc

    loads = []
    for i in range(LOADS):
        cp = pltpu.make_async_copy(
            down_ref.at[pl.ds(i * span, span)], down_vm.at[pl.ds(i * span, span)], load_sem.at[0, i])
        cp.start()
    own = []
    for q in range(Q):
        cp = pltpu.make_async_copy(
            x_ref.at[:, pl.ds(q * kq, kq)], gathered.at[q, pl.ds(pl.multiple_of(me * rows, rows), rows)], own_sem.at[q])
        cp.start()
        own.append(cp)
    own_block = pltpu.make_async_copy(
        x_ref.at[:, pl.ds(pl.multiple_of(me * feat, feat), feat)],
        block.at[pl.ds(pl.multiple_of(me * rows, rows), rows)], own_sem.at[Q])
    own_block.start()
    for i in range(LOADS):
        pltpu.make_async_copy(
            up_ref.at[pl.ds(i * span, span)], up_vm.at[pl.ds(i * span, span)], load_sem.at[1, i]).start()
    for q in range(Q):
        pltpu.make_async_copy(
            w_ref.at[pl.ds(q * kq, kq)], w_vm.at[pl.ds(q * kq, kq)], w_sem.at[q]).start()

    barrier = pltpu.get_barrier_semaphore()
    for d in range(1, N):
        pl.semaphore_signal(barrier, inc=1, device_id={"tensor": (me + d) % N}, device_id_type=MESH)
    pl.semaphore_wait(barrier, N - 1)

    sends = []

    def send(src, dst, ssem, rsem, target, cond=None):
        cp = pltpu.make_async_remote_copy(
            src_ref=src, dst_ref=dst, send_sem=ssem, recv_sem=rsem,
            device_id={"tensor": target}, device_id_type=MESH)
        if cond is None:
            cp.start()
        else:
            pl.when(cond)(cp.start)
        sends.append((cp, cond))

    for d in range(1, N):
        to = (me + d) % N
        send(x_ref.at[:, pl.ds(pl.multiple_of(to * feat, feat), feat)],
             block.at[pl.ds(pl.multiple_of(me * rows, rows), rows)],
             a2a_send.at[d], a2a_recv.at[d], to)

    def place(q, origin):
        return gathered.at[q, pl.ds(pl.multiple_of(origin * rows, rows), rows)]

    for q in range(Q):
        src = x_ref.at[:, pl.ds(q * kq, kq)]
        dst = place(q, me)
        send(src, dst, z_send.at[0, q], recv.at[q, me], dev(z + 1, y, c), z < Z - 1)
        send(src, dst, z_send.at[1, q], recv.at[q, me], dev(z - 1, y, c), z > 0)
        send(src, dst, y_send.at[0, q], recv.at[q, me], dev(z, 1 - y, c))
        send(src, dst, c_send.at[0, q], recv.at[q, me], dev(z, y, 1 - c))

    far = [None, z + 1 - 2 * (z % 2), 2 - z // 2, 3 - 3 * (z // 2)]
    hop = [None, 3 - z, 3 * (z - 1), 3 * (z - 1)]
    middle = (z == 1) | (z == 2)

    def wait_in(q, origin):
        ref = place(q, origin)
        pltpu.make_async_remote_copy(
            src_ref=ref, dst_ref=ref, send_sem=y_send.at[0, q], recv_sem=recv.at[q, origin],
            device_id={"tensor": dev(z, y, 1 - c)}, device_id_type=MESH).wait_recv()

    def z_event(d, q):
        origin = dev(far[d], y, c)
        wait_in(q, origin)
        ref = place(q, origin)
        send(ref, ref, z_send.at[1 + d, q], recv.at[q, origin], dev(hop[d], y, c), middle)
        send(ref, ref, y_send.at[d, q], recv.at[q, origin], dev(z, 1 - y, c))
        send(ref, ref, c_send.at[d, q], recv.at[q, origin], dev(z, y, 1 - c))

    def y_event(d, q):
        origin = dev(z if d == 0 else far[d], 1 - y, c)
        wait_in(q, origin)
        ref = place(q, origin)
        send(ref, ref, c_send.at[4 + d, q], recv.at[q, origin], dev(z, y, 1 - c))

    picks = picks_ref[...]

    def look(e, slot):
        return jnp.where(picks == e, index_ref[e], slot)

    slot = lax.fori_loop(0, stored, look, jnp.zeros_like(picks), unroll=8)

    own_block.wait()
    for d in range(1, N):
        frm = (me + N - d) % N
        ref = block.at[pl.ds(pl.multiple_of(frm * rows, rows), rows)]
        pltpu.make_async_remote_copy(
            src_ref=ref, dst_ref=ref, send_sem=a2a_send.at[d], recv_sem=a2a_recv.at[d],
            device_id={"tensor": frm}, device_id_type=MESH).wait_recv()

    def load_wait(which, src, vm, i):
        at = pl.ds(pl.multiple_of(i * span, span), span)
        pltpu.make_async_copy(src.at[at], vm.at[at], load_sem.at[which, i]).wait()

    slot0, slot1 = slot[0:1], slot[1:2]

    def shrink(i, carry):
        load_wait(0, down_ref, down_vm, i)
        at = pl.ds(pl.multiple_of(i * span, span), span)
        res = lax.dot_general(down_vm[at, :], block[...], (((1,), (1,)), ((), ())),
                              preferred_element_type=jnp.float32)
        first, second = carry
        s0, s1 = slot0 - i * per, slot1 - i * per
        for e in range(per):
            part = res[e * rank:(e + 1) * rank]
            first = jnp.where(s0 == e, part, first)
            second = jnp.where(s1 == e, part, second)
        return first, second

    zero = jnp.zeros((rank, tokens), jnp.float32)
    carry = lax.fori_loop(0, LOADS // 2, shrink, (zero, zero))
    for q in range(Q):
        z_event(1, q)
    carry = lax.fori_loop(LOADS // 2, LOADS, shrink, carry)
    each = 2 * rank // N
    for k in range(2):
        for j in range(N // 2):
            partial[k * (N // 2) + j] = carry[k][j * each:(j + 1) * each]
    pieces[0] = partial[me]
    for d in range(1, N):
        to = (me + d) % N
        send(partial.at[to], pieces.at[d], rs_send.at[d], rs_recv.at[d], to)
    for q in range(Q):
        y_event(0, q)
    for q in range(Q):
        z_event(2, q)
    for d in range(1, N):
        pltpu.make_async_remote_copy(
            src_ref=pieces.at[d], dst_ref=pieces.at[d], send_sem=rs_send.at[d], recv_sem=rs_recv.at[d],
            device_id={"tensor": (me + N - d) % N}, device_id_type=MESH).wait_recv()
    mine = pieces[0]
    for d in range(1, N):
        mine = mine + pieces[d]
    half = tokens // 2
    reduced[me] = jnp.concatenate([mine[:, :half], mine[:, half:]], axis=0).astype(jnp.bfloat16)
    for d in range(1, N):
        to = (me + d) % N
        send(reduced.at[me], reduced.at[me], ag_send.at[d], ag_recv.at[d], to)
    for q in range(Q):
        y_event(1, q)
    for d in range(1, N):
        frm = (me + N - d) % N
        pltpu.make_async_remote_copy(
            src_ref=reduced.at[frm], dst_ref=reduced.at[frm], send_sem=ag_send.at[d], recv_sem=ag_recv.at[d],
            device_id={"tensor": frm}, device_id_type=MESH).wait_recv()

    gates = gates_ref[...]
    upper = (lax.broadcasted_iota(jnp.int32, (2 * rank, tokens), 0) >= rank).astype(jnp.int32)
    vectors, marks = [], []
    for k in range(2):
        flat = []
        for j in range(N // 2):
            piece = reduced[k * (N // 2) + j].astype(jnp.float32)
            flat.append(jnp.concatenate([piece[:each], piece[each:]], axis=1))
        flat = jnp.concatenate(flat + flat, axis=0) * gates[k:k + 1]
        vectors.append(jnp.transpose(flat).astype(jnp.bfloat16))
        mark = (slot[k:k + 1] - upper).astype(jnp.float32)
        marks.append(jnp.transpose(mark).astype(jnp.bfloat16))

    total[...] = jnp.zeros_like(total)

    def expand(i, _):
        load_wait(1, up_ref, up_vm, i)
        at = pl.ds(pl.multiple_of(i * span, span), span)
        base = (i * per).astype(jnp.float32).astype(jnp.bfloat16)
        m0, m1 = marks[0] - base, marks[1] - base
        nil = jnp.zeros_like(vectors[0])
        for j in range(per // 2):
            v = jnp.where(m0 == 2 * j, vectors[0], jnp.where(m1 == 2 * j, vectors[1], nil))
            mixed_rows[:, j * 2 * rank:(j + 1) * 2 * rank] = v
        total[...] += jnp.dot(mixed_rows[...], up_vm[at, :], preferred_element_type=jnp.float32)
        return 0

    lax.fori_loop(0, LOADS // 2, expand, 0)
    for q in range(Q):
        z_event(3, q)
    for q in range(Q):
        y_event(2, q)
    lax.fori_loop(LOADS // 2, LOADS, expand, 0)
    for q in range(Q):
        y_event(3, q)

    for q in range(Q):
        own[q].wait()
        for zz in [z] + far[1:]:
            for yy in (y, 1 - y):
                wait_in(q, dev(zz, yy, 1 - c))
        pltpu.make_async_copy(
            w_ref.at[pl.ds(q * kq, kq)], w_vm.at[pl.ds(q * kq, kq)], w_sem.at[q]).wait()
        part = total[...] + jnp.dot(
            gathered[q], w_vm[pl.ds(q * kq, kq), :], preferred_element_type=jnp.float32)
        if q < Q - 1:
            total[...] = part
        else:
            out_ref[...] = part.astype(out_ref.dtype)

    for cp, cond in sends:
        if cond is None:
            cp.wait_send()
        else:
            pl.when(cond)(cp.wait_send)


def by_kernel(rows, weight, down, up, picks, gates, index):
    stored, feat, rank = down.shape
    tokens = picks.shape[0]
    width = weight.shape[0]
    columns = weight.shape[1]
    span = stored // LOADS * rank
    any_ = pl.BlockSpec(memory_space=pl.ANY)
    vm = pl.BlockSpec(memory_space=pltpu.VMEM)
    dma = pltpu.SemaphoreType.DMA
    return pl.pallas_call(
        fused,
        out_shape=jax.ShapeDtypeStruct((tokens, columns), jnp.bfloat16),
        in_specs=[any_, any_, any_, any_, vm, vm, pl.BlockSpec(memory_space=pltpu.SMEM)],
        out_specs=vm,
        scratch_shapes=[
            pltpu.VMEM((Q, tokens, width // Q), jnp.bfloat16),
            pltpu.VMEM((tokens, feat), jnp.bfloat16),
            pltpu.VMEM((width, columns), jnp.bfloat16),
            pltpu.VMEM((stored * rank, feat), jnp.bfloat16),
            pltpu.VMEM((stored * rank, columns), jnp.bfloat16),
            pltpu.VMEM((8, 128), jnp.float32),
            pltpu.VMEM((tokens, span), jnp.bfloat16),
            pltpu.VMEM((N, 2 * rank // N, tokens), jnp.float32),
            pltpu.VMEM((N, 2 * rank // N, tokens), jnp.float32),
            pltpu.VMEM((N, 4 * rank // N, tokens // 2), jnp.bfloat16),
            pltpu.VMEM((tokens, columns), jnp.float32),
            dma((2, LOADS)), dma((Q,)), dma((Q + 1,)), dma((N,)), dma((N,)),
            dma((5, Q)), dma((4, Q)), dma((8, Q)), dma((Q, N)),
            dma((N,)), dma((N,)), dma((N,)), dma((N,)),
        ],
        compiler_params=pltpu.CompilerParams(
            collective_id=0, has_side_effects=True, vmem_limit_bytes=60 * 2**20),
        cost_estimate=pl.CostEstimate(
            flops=2 * tokens * columns * (width + 2 * stored * rank),
            bytes_accessed=2 * (weight.size + down.size + up.size), transcendentals=0),
    )(
        rows, weight, jnp.swapaxes(down, 1, 2).reshape(stored * rank, feat),
        up.reshape(stored * rank, columns), picks.T, gates.T, index,
    )


def routing(picks, gates, adapter_storage_index, storage_count, most):
    chosen = picks.reshape(-1)
    slot_of = jnp.take(adapter_storage_index, chosen)
    onehot = (slot_of[:, None] == jnp.arange(storage_count, dtype=jnp.int32)[None, :]).astype(
        jnp.int32
    )
    order_in = jnp.sum((jnp.cumsum(onehot, axis=0) - onehot) * onehot, axis=1)
    position = slot_of * most + order_in
    token_ids = jnp.arange(chosen.shape[0], dtype=jnp.int32) // 2
    token_of = jnp.zeros((storage_count * most,), jnp.int32).at[position].set(token_ids)
    token_gate_weight = (
        jnp.zeros((storage_count * most,), jnp.float32).at[position].set(gates.reshape(-1))
    )
    live = (
        jnp.zeros((storage_count * most,), jnp.float32)
        .at[position]
        .set(jnp.ones_like(gates.reshape(-1)))
    )
    return (token_of, token_gate_weight, live)


def by_collectives(rows, weight, down, up, picks, gates, index):
    storage_count = down.shape[0]
    most = max(2, 8 * picks.shape[0] // storage_count)
    columns = weight.shape[1]
    gathered = lax.all_gather(rows, "tensor", axis=0, tiled=True)
    base = jnp.dot(gathered, weight, preferred_element_type=jnp.float32)
    own_block = lax.dynamic_slice_in_dim(gathered, lax.axis_index("tensor") * columns, columns, 1)
    token_of, token_gate_weight, live = routing(picks, gates, index, storage_count, most)
    routed = (own_block[token_of] * live[:, None].astype(own_block.dtype)).reshape(
        storage_count, most, columns
    )
    partial = jnp.einsum("kit,ktn->kin", routed, down, preferred_element_type=jnp.float32)
    reduced = lax.psum(partial, "tensor").astype(jnp.bfloat16)
    expanded = jnp.einsum("hou,hut->hot", reduced, up, preferred_element_type=jnp.float32)
    expanded = expanded * token_gate_weight.reshape(storage_count, most)[:, :, None]
    total = base.at[token_of].add(expanded.reshape(storage_count * most, columns))
    return total.astype(jnp.bfloat16)


def solution(mesh):
    placed = (
        P(("groups", "tensor"), None),
        P(None, "tensor"),
        P(None, "tensor", None),
        P(None, None, "tensor"),
        P("groups", None),
        P("groups", None),
        P(),
    )
    body = by_kernel if mesh.shape["tensor"] == N else by_collectives
    return jax.shard_map(
        body, mesh=mesh, in_specs=placed, out_specs=P("groups", "tensor"), check_vma=False
    )
```

```python
import functools

import jax
import jax.numpy as jnp
from jax import lax
from jax.experimental import pallas as pl
from jax.experimental.pallas import tpu as pltpu
from jax.sharding import PartitionSpec as P

MESH = pl.DeviceIdType.MESH
Z, Y, C = 4, 2, 2
N = Z * Y * C
Q = 4
LOADS = 8


def fused(
    x_ref, w_ref, down_ref, up_ref, picks_ref, gates_ref, index_ref, out_ref,
    gathered, block, w_vm, down_vm, up_vm, mixed_rows, partial, pieces, reduced, total,
    load_sem, w_sem, own_sem, a2a_send, a2a_recv, z_send, y_send, c_send, recv,
    rs_send, rs_recv, ag_send, ag_recv,
):
    rows = x_ref.shape[0]
    tokens = rows * N
    feat = block.shape[1]
    kq = gathered.shape[2]
    stored = index_ref.shape[0]
    rank = down_ref.shape[0] // stored
    per = stored // LOADS
    span = per * rank
    me = lax.axis_index("tensor")
    z = me // (Y * C)
    yc = me % (Y * C)
    y = yc // C
    c = yc % C

    def dev(zz, yy, cc):
        return (zz * Y + yy) * C + cc

    own = []
    for q in range(Q):
        cp = pltpu.make_async_copy(
            x_ref.at[:, pl.ds(q * kq, kq)], gathered.at[q, pl.ds(pl.multiple_of(me * rows, rows), rows)], own_sem.at[q])
        cp.start()
        own.append(cp)
    own_block = pltpu.make_async_copy(
        x_ref.at[:, pl.ds(pl.multiple_of(me * feat, feat), feat)],
        block.at[pl.ds(pl.multiple_of(me * rows, rows), rows)], own_sem.at[Q])
    own_block.start()
    for i in range(LOADS):
        pltpu.make_async_copy(
            down_ref.at[pl.ds(i * span, span)], down_vm.at[pl.ds(i * span, span)], load_sem.at[0, i]).start()

    barrier = pltpu.get_barrier_semaphore()
    for d in range(1, N):
        pl.semaphore_signal(barrier, inc=1, device_id={"tensor": (me + d) % N}, device_id_type=MESH)
    pl.semaphore_wait(barrier, N - 1)

    sends = []

    def send(src, dst, ssem, rsem, target, cond=None):
        cp = pltpu.make_async_remote_copy(
            src_ref=src, dst_ref=dst, send_sem=ssem, recv_sem=rsem,
            device_id={"tensor": target}, device_id_type=MESH)
        if cond is None:
            cp.start()
        else:
            pl.when(cond)(cp.start)
        sends.append((cp, cond))

    for d in range(1, N):
        to = (me + d) % N
        send(x_ref.at[:, pl.ds(pl.multiple_of(to * feat, feat), feat)],
             block.at[pl.ds(pl.multiple_of(me * rows, rows), rows)],
             a2a_send.at[d], a2a_recv.at[d], to)

    def place(q, origin):
        return gathered.at[q, pl.ds(pl.multiple_of(origin * rows, rows), rows)]

    for q in range(Q):
        src = x_ref.at[:, pl.ds(q * kq, kq)]
        dst = place(q, me)
        send(src, dst, z_send.at[0, q], recv.at[q, me], dev(z + 1, y, c), z < Z - 1)
        send(src, dst, z_send.at[1, q], recv.at[q, me], dev(z - 1, y, c), z > 0)
        send(src, dst, y_send.at[0, q], recv.at[q, me], dev(z, 1 - y, c))
        send(src, dst, c_send.at[0, q], recv.at[q, me], dev(z, y, 1 - c))

    far = [None, z + 1 - 2 * (z % 2), 2 - z // 2, 3 - 3 * (z // 2)]
    hop = [None, 3 - z, 3 * (z - 1), 3 * (z - 1)]
    middle = (z == 1) | (z == 2)

    def wait_in(q, origin):
        ref = place(q, origin)
        pltpu.make_async_remote_copy(
            src_ref=ref, dst_ref=ref, send_sem=y_send.at[0, q], recv_sem=recv.at[q, origin],
            device_id={"tensor": dev(z, y, 1 - c)}, device_id_type=MESH).wait_recv()

    def z_event(d, q):
        origin = dev(far[d], y, c)
        wait_in(q, origin)
        ref = place(q, origin)
        send(ref, ref, z_send.at[1 + d, q], recv.at[q, origin], dev(hop[d], y, c), middle)
        send(ref, ref, y_send.at[d, q], recv.at[q, origin], dev(z, 1 - y, c))
        send(ref, ref, c_send.at[d, q], recv.at[q, origin], dev(z, y, 1 - c))

    def y_event(d, q):
        origin = dev(z if d == 0 else far[d], 1 - y, c)
        wait_in(q, origin)
        ref = place(q, origin)
        send(ref, ref, c_send.at[4 + d, q], recv.at[q, origin], dev(z, y, 1 - c))

    picks = picks_ref[...]

    def look(e, slot):
        return jnp.where(picks == e, index_ref[e], slot)

    slot = lax.fori_loop(0, stored, look, jnp.zeros_like(picks), unroll=8)

    own_block.wait()
    for d in range(1, N):
        frm = (me + N - d) % N
        ref = block.at[pl.ds(pl.multiple_of(frm * rows, rows), rows)]
        pltpu.make_async_remote_copy(
            src_ref=ref, dst_ref=ref, send_sem=a2a_send.at[d], recv_sem=a2a_recv.at[d],
            device_id={"tensor": frm}, device_id_type=MESH).wait_recv()

    def load_wait(which, src, vm, i):
        at = pl.ds(pl.multiple_of(i * span, span), span)
        pltpu.make_async_copy(src.at[at], vm.at[at], load_sem.at[which, i]).wait()

    slot0, slot1 = slot[0:1], slot[1:2]

    def shrink(i, carry):
        load_wait(0, down_ref, down_vm, i)
        at = pl.ds(pl.multiple_of(i * span, span), span)
        pltpu.make_async_copy(up_ref.at[at], up_vm.at[at], load_sem.at[1, i]).start()
        res = lax.dot_general(down_vm[at, :], block[...], (((1,), (1,)), ((), ())),
                              preferred_element_type=jnp.float32)
        first, second = carry
        s0, s1 = slot0 - i * per, slot1 - i * per
        for e in range(per):
            part = res[e * rank:(e + 1) * rank]
            first = jnp.where(s0 == e, part, first)
            second = jnp.where(s1 == e, part, second)
        return first, second

    zero = jnp.zeros((rank, tokens), jnp.float32)
    carry = lax.fori_loop(0, LOADS // 2, shrink, (zero, zero))
    for q in range(Q):
        z_event(1, q)
        carry = lax.fori_loop(LOADS // 2 + q, LOADS // 2 + q + 1, shrink, carry)
    for q in range(Q):
        pltpu.make_async_copy(
            w_ref.at[pl.ds(q * kq, kq)], w_vm.at[pl.ds(q * kq, kq)], w_sem.at[q]).start()
    each = 2 * rank // N
    for k in range(2):
        for j in range(N // 2):
            partial[k * (N // 2) + j] = carry[k][j * each:(j + 1) * each]
    pieces[0] = partial[me]
    for d in range(1, N):
        to = (me + d) % N
        send(partial.at[to], pieces.at[d], rs_send.at[d], rs_recv.at[d], to)
    for q in range(Q):
        y_event(0, q)
    for q in range(Q):
        z_event(2, q)
    for d in range(1, N):
        pltpu.make_async_remote_copy(
            src_ref=pieces.at[d], dst_ref=pieces.at[d], send_sem=rs_send.at[d], recv_sem=rs_recv.at[d],
            device_id={"tensor": (me + N - d) % N}, device_id_type=MESH).wait_recv()
    mine = pieces[0]
    for d in range(1, N):
        mine = mine + pieces[d]
    half = tokens // 2
    reduced[me] = jnp.concatenate([mine[:, :half], mine[:, half:]], axis=0).astype(jnp.bfloat16)
    for d in range(1, N):
        to = (me + d) % N
        send(reduced.at[me], reduced.at[me], ag_send.at[d], ag_recv.at[d], to)
    for q in range(Q):
        y_event(1, q)
        z_event(3, q)
    for d in range(1, N):
        frm = (me + N - d) % N
        pltpu.make_async_remote_copy(
            src_ref=reduced.at[frm], dst_ref=reduced.at[frm], send_sem=ag_send.at[d], recv_sem=ag_recv.at[d],
            device_id={"tensor": frm}, device_id_type=MESH).wait_recv()

    gates = gates_ref[...]
    upper = (lax.broadcasted_iota(jnp.int32, (2 * rank, tokens), 0) >= rank).astype(jnp.int32)
    vectors, marks = [], []
    for k in range(2):
        flat = []
        for j in range(N // 2):
            piece = reduced[k * (N // 2) + j].astype(jnp.float32)
            flat.append(jnp.concatenate([piece[:each], piece[each:]], axis=1))
        flat = jnp.concatenate(flat + flat, axis=0) * gates[k:k + 1]
        vectors.append(jnp.transpose(flat).astype(jnp.bfloat16))
        mark = (slot[k:k + 1] - upper).astype(jnp.float32)
        marks.append(jnp.transpose(mark).astype(jnp.bfloat16))

    total[...] = jnp.zeros_like(total)

    def expand(i, _):
        load_wait(1, up_ref, up_vm, i)
        at = pl.ds(pl.multiple_of(i * span, span), span)
        base = (i * per).astype(jnp.float32).astype(jnp.bfloat16)
        m0, m1 = marks[0] - base, marks[1] - base
        nil = jnp.zeros_like(vectors[0])
        for j in range(per // 2):
            v = jnp.where(m0 == 2 * j, vectors[0], jnp.where(m1 == 2 * j, vectors[1], nil))
            mixed_rows[:, j * 2 * rank:(j + 1) * 2 * rank] = v
        total[...] += jnp.dot(mixed_rows[...], up_vm[at, :], preferred_element_type=jnp.float32)
        return 0

    lax.fori_loop(0, LOADS // 2, expand, 0)
    for q in range(Q):
        y_event(2, q)
    lax.fori_loop(LOADS // 2, LOADS, expand, 0)
    for q in range(Q):
        y_event(3, q)

    for q in range(Q):
        own[q].wait()
        for zz in [z] + far[1:]:
            for yy in (y, 1 - y):
                wait_in(q, dev(zz, yy, 1 - c))
        pltpu.make_async_copy(
            w_ref.at[pl.ds(q * kq, kq)], w_vm.at[pl.ds(q * kq, kq)], w_sem.at[q]).wait()
        part = total[...] + jnp.dot(
            gathered[q], w_vm[pl.ds(q * kq, kq), :], preferred_element_type=jnp.float32)
        if q < Q - 1:
            total[...] = part
        else:
            out_ref[...] = part.astype(out_ref.dtype)

    for cp, cond in sends:
        if cond is None:
            cp.wait_send()
        else:
            pl.when(cond)(cp.wait_send)


def by_kernel(rows, weight, down, up, picks, gates, index):
    stored, feat, rank = down.shape
    tokens = picks.shape[0]
    width = weight.shape[0]
    columns = weight.shape[1]
    span = stored // LOADS * rank
    any_ = pl.BlockSpec(memory_space=pl.ANY)
    vm = pl.BlockSpec(memory_space=pltpu.VMEM)
    dma = pltpu.SemaphoreType.DMA
    return pl.pallas_call(
        fused,
        out_shape=jax.ShapeDtypeStruct((tokens, columns), jnp.bfloat16),
        in_specs=[any_, any_, any_, any_, vm, vm, pl.BlockSpec(memory_space=pltpu.SMEM)],
        out_specs=vm,
        scratch_shapes=[
            pltpu.VMEM((Q, tokens, width // Q), jnp.bfloat16),
            pltpu.VMEM((tokens, feat), jnp.bfloat16),
            pltpu.VMEM((width, columns), jnp.bfloat16),
            pltpu.VMEM((stored * rank, feat), jnp.bfloat16),
            pltpu.VMEM((stored * rank, columns), jnp.bfloat16),
            pltpu.VMEM((tokens, span), jnp.bfloat16),
            pltpu.VMEM((N, 2 * rank // N, tokens), jnp.float32),
            pltpu.VMEM((N, 2 * rank // N, tokens), jnp.float32),
            pltpu.VMEM((N, 4 * rank // N, tokens // 2), jnp.bfloat16),
            pltpu.VMEM((tokens, columns), jnp.float32),
            dma((2, LOADS)), dma((Q,)), dma((Q + 1,)), dma((N,)), dma((N,)),
            dma((5, Q)), dma((4, Q)), dma((8, Q)), dma((Q, N)),
            dma((N,)), dma((N,)), dma((N,)), dma((N,)),
        ],
        compiler_params=pltpu.CompilerParams(
            collective_id=0, has_side_effects=True, vmem_limit_bytes=60 * 2**20),
        cost_estimate=pl.CostEstimate(
            flops=2 * tokens * columns * (width + 2 * stored * rank),
            bytes_accessed=2 * (weight.size + down.size + up.size), transcendentals=0),
    )(
        rows, weight, jnp.swapaxes(down, 1, 2).reshape(stored * rank, feat),
        up.reshape(stored * rank, columns), picks.T, gates.T, index,
    )


def routing(picks, gates, adapter_storage_index, storage_count, most):
    chosen = picks.reshape(-1)
    slot_of = jnp.take(adapter_storage_index, chosen)
    onehot = (slot_of[:, None] == jnp.arange(storage_count, dtype=jnp.int32)[None, :]).astype(
        jnp.int32
    )
    order_in = jnp.sum((jnp.cumsum(onehot, axis=0) - onehot) * onehot, axis=1)
    position = slot_of * most + order_in
    token_ids = jnp.arange(chosen.shape[0], dtype=jnp.int32) // 2
    token_of = jnp.zeros((storage_count * most,), jnp.int32).at[position].set(token_ids)
    token_gate_weight = (
        jnp.zeros((storage_count * most,), jnp.float32).at[position].set(gates.reshape(-1))
    )
    live = (
        jnp.zeros((storage_count * most,), jnp.float32)
        .at[position]
        .set(jnp.ones_like(gates.reshape(-1)))
    )
    return (token_of, token_gate_weight, live)


def by_collectives(rows, weight, down, up, picks, gates, index):
    storage_count = down.shape[0]
    most = max(2, 8 * picks.shape[0] // storage_count)
    columns = weight.shape[1]
    gathered = lax.all_gather(rows, "tensor", axis=0, tiled=True)
    base = jnp.dot(gathered, weight, preferred_element_type=jnp.float32)
    own_block = lax.dynamic_slice_in_dim(gathered, lax.axis_index("tensor") * columns, columns, 1)
    token_of, token_gate_weight, live = routing(picks, gates, index, storage_count, most)
    routed = (own_block[token_of] * live[:, None].astype(own_block.dtype)).reshape(
        storage_count, most, columns
    )
    partial = jnp.einsum("kit,ktn->kin", routed, down, preferred_element_type=jnp.float32)
    reduced = lax.psum(partial, "tensor").astype(jnp.bfloat16)
    expanded = jnp.einsum("hou,hut->hot", reduced, up, preferred_element_type=jnp.float32)
    expanded = expanded * token_gate_weight.reshape(storage_count, most)[:, :, None]
    total = base.at[token_of].add(expanded.reshape(storage_count * most, columns))
    return total.astype(jnp.bfloat16)


def solution(mesh):
    placed = (
        P(("groups", "tensor"), None),
        P(None, "tensor"),
        P(None, "tensor", None),
        P(None, None, "tensor"),
        P("groups", None),
        P("groups", None),
        P(),
    )
    body = by_kernel if mesh.shape["tensor"] == N else by_collectives
    return jax.shard_map(
        body, mesh=mesh, in_specs=placed, out_specs=P("groups", "tensor"), check_vma=False
    )
```

```python
import functools

import jax
import jax.numpy as jnp
from jax import lax
from jax.experimental import pallas as pl
from jax.experimental.pallas import tpu as pltpu
from jax.sharding import PartitionSpec as P

MESH = pl.DeviceIdType.MESH
Z, Y, C = 4, 2, 2
N = Z * Y * C
Q = 4
LOADS = 8


def fused(
    x_ref, w_ref, down_ref, up_ref, picks_ref, gates_ref, index_ref, out_ref,
    gathered, block, w_vm, down_vm, up_vm, mixed_rows, partial, pieces, reduced, total,
    load_sem, w_sem, own_sem, a2a_send, a2a_recv, z_send, y_send, c_send, recv,
    rs_send, rs_recv, ag_send, ag_recv,
):
    rows = x_ref.shape[0]
    tokens = rows * N
    feat = block.shape[1]
    kq = gathered.shape[2]
    stored = index_ref.shape[0]
    rank = down_ref.shape[0] // stored
    per = stored // LOADS
    span = per * rank
    me = lax.axis_index("tensor")
    z = me // (Y * C)
    yc = me % (Y * C)
    y = yc // C
    c = yc % C

    def dev(zz, yy, cc):
        return (zz * Y + yy) * C + cc

    own = []
    for q in range(Q):
        cp = pltpu.make_async_copy(
            x_ref.at[:, pl.ds(q * kq, kq)], gathered.at[q, pl.ds(pl.multiple_of(me * rows, rows), rows)], own_sem.at[q])
        cp.start()
        own.append(cp)
    own_block = pltpu.make_async_copy(
        x_ref.at[:, pl.ds(pl.multiple_of(me * feat, feat), feat)],
        block.at[pl.ds(pl.multiple_of(me * rows, rows), rows)], own_sem.at[Q])
    own_block.start()
    for i in range(LOADS):
        pltpu.make_async_copy(
            down_ref.at[pl.ds(i * span, span)], down_vm.at[pl.ds(i * span, span)], load_sem.at[0, i]).start()

    barrier = pltpu.get_barrier_semaphore()
    for d in range(1, N):
        pl.semaphore_signal(barrier, inc=1, device_id={"tensor": (me + d) % N}, device_id_type=MESH)
    pl.semaphore_wait(barrier, N - 1)

    sends = []

    def send(src, dst, ssem, rsem, target, cond=None):
        cp = pltpu.make_async_remote_copy(
            src_ref=src, dst_ref=dst, send_sem=ssem, recv_sem=rsem,
            device_id={"tensor": target}, device_id_type=MESH)
        if cond is None:
            cp.start()
        else:
            pl.when(cond)(cp.start)
        sends.append((cp, cond))

    for d in range(1, N):
        to = (me + d) % N
        send(x_ref.at[:, pl.ds(pl.multiple_of(to * feat, feat), feat)],
             block.at[pl.ds(pl.multiple_of(me * rows, rows), rows)],
             a2a_send.at[d], a2a_recv.at[d], to)

    def place(q, origin):
        return gathered.at[q, pl.ds(pl.multiple_of(origin * rows, rows), rows)]

    for q in range(Q):
        src = x_ref.at[:, pl.ds(q * kq, kq)]
        dst = place(q, me)
        send(src, dst, z_send.at[0, q], recv.at[q, me], dev(z + 1, y, c), z < Z - 1)
        send(src, dst, z_send.at[1, q], recv.at[q, me], dev(z - 1, y, c), z > 0)
        send(src, dst, y_send.at[0, q], recv.at[q, me], dev(z, 1 - y, c))
        send(src, dst, c_send.at[0, q], recv.at[q, me], dev(z, y, 1 - c))

    far = [None, z + 1 - 2 * (z % 2), 2 - z // 2, 3 - 3 * (z // 2)]
    hop = [None, 3 - z, 3 * (z - 1), 3 * (z - 1)]
    middle = (z == 1) | (z == 2)

    def wait_in(q, origin):
        ref = place(q, origin)
        pltpu.make_async_remote_copy(
            src_ref=ref, dst_ref=ref, send_sem=y_send.at[0, q], recv_sem=recv.at[q, origin],
            device_id={"tensor": dev(z, y, 1 - c)}, device_id_type=MESH).wait_recv()

    def z_event(d, q):
        origin = dev(far[d], y, c)
        wait_in(q, origin)
        ref = place(q, origin)
        send(ref, ref, z_send.at[1 + d, q], recv.at[q, origin], dev(hop[d], y, c), middle)
        send(ref, ref, y_send.at[d, q], recv.at[q, origin], dev(z, 1 - y, c))
        send(ref, ref, c_send.at[d, q], recv.at[q, origin], dev(z, y, 1 - c))

    def y_event(d, q):
        origin = dev(z if d == 0 else far[d], 1 - y, c)
        wait_in(q, origin)
        ref = place(q, origin)
        send(ref, ref, c_send.at[4 + d, q], recv.at[q, origin], dev(z, y, 1 - c))

    picks = picks_ref[...]

    def look(e, slot):
        return jnp.where(picks == e, index_ref[e], slot)

    slot = lax.fori_loop(0, stored, look, jnp.zeros_like(picks), unroll=8)

    own_block.wait()
    for d in range(1, N):
        frm = (me + N - d) % N
        ref = block.at[pl.ds(pl.multiple_of(frm * rows, rows), rows)]
        pltpu.make_async_remote_copy(
            src_ref=ref, dst_ref=ref, send_sem=a2a_send.at[d], recv_sem=a2a_recv.at[d],
            device_id={"tensor": frm}, device_id_type=MESH).wait_recv()

    def load_wait(which, src, vm, i):
        at = pl.ds(pl.multiple_of(i * span, span), span)
        pltpu.make_async_copy(src.at[at], vm.at[at], load_sem.at[which, i]).wait()

    slot0, slot1 = slot[0:1], slot[1:2]

    def shrink(i, carry):
        load_wait(0, down_ref, down_vm, i)
        at = pl.ds(pl.multiple_of(i * span, span), span)
        pltpu.make_async_copy(up_ref.at[at], up_vm.at[at], load_sem.at[1, i]).start()
        res = lax.dot_general(down_vm[at, :], block[...], (((1,), (1,)), ((), ())),
                              preferred_element_type=jnp.float32)
        first, second = carry
        s0, s1 = slot0 - i * per, slot1 - i * per
        for e in range(per):
            part = res[e * rank:(e + 1) * rank]
            first = jnp.where(s0 == e, part, first)
            second = jnp.where(s1 == e, part, second)
        return first, second

    zero = jnp.zeros((rank, tokens), jnp.float32)
    carry = lax.fori_loop(0, LOADS // 2, shrink, (zero, zero))
    for q in range(Q):
        z_event(1, q)
        carry = lax.fori_loop(LOADS // 2 + q, LOADS // 2 + q + 1, shrink, carry)
    for q in range(Q):
        pltpu.make_async_copy(
            w_ref.at[pl.ds(q * kq, kq)], w_vm.at[pl.ds(q * kq, kq)], w_sem.at[q]).start()
    each = 2 * rank // N
    half = tokens // 2
    for k in range(2):
        for j in range(N // 2):
            part = carry[k][j * each:(j + 1) * each]
            partial[k * (N // 2) + j] = jnp.concatenate(
                [part[:, :half], part[:, half:]], axis=0).astype(jnp.bfloat16)
    pieces[0] = partial[me]
    for d in range(1, N):
        to = (me + d) % N
        send(partial.at[to], pieces.at[d], rs_send.at[d], rs_recv.at[d], to)
    for q in range(Q):
        y_event(0, q)
    for q in range(Q):
        z_event(2, q)
    for d in range(1, N):
        pltpu.make_async_remote_copy(
            src_ref=pieces.at[d], dst_ref=pieces.at[d], send_sem=rs_send.at[d], recv_sem=rs_recv.at[d],
            device_id={"tensor": (me + N - d) % N}, device_id_type=MESH).wait_recv()
    mine = pieces[0].astype(jnp.float32)
    for d in range(1, N):
        mine = mine + pieces[d].astype(jnp.float32)
    reduced[me] = mine.astype(jnp.bfloat16)
    for d in range(1, N):
        to = (me + d) % N
        send(reduced.at[me], reduced.at[me], ag_send.at[d], ag_recv.at[d], to)
    for q in range(Q):
        y_event(1, q)
        z_event(3, q)
    for d in range(1, N):
        frm = (me + N - d) % N
        pltpu.make_async_remote_copy(
            src_ref=reduced.at[frm], dst_ref=reduced.at[frm], send_sem=ag_send.at[d], recv_sem=ag_recv.at[d],
            device_id={"tensor": frm}, device_id_type=MESH).wait_recv()

    gates = gates_ref[...]
    upper = (lax.broadcasted_iota(jnp.int32, (2 * rank, tokens), 0) >= rank).astype(jnp.int32)
    vectors, marks = [], []
    for k in range(2):
        flat = []
        for j in range(N // 2):
            piece = reduced[k * (N // 2) + j].astype(jnp.float32)
            flat.append(jnp.concatenate([piece[:each], piece[each:]], axis=1))
        flat = jnp.concatenate(flat + flat, axis=0) * gates[k:k + 1]
        vectors.append(jnp.transpose(flat).astype(jnp.bfloat16))
        mark = (slot[k:k + 1] - upper).astype(jnp.float32)
        marks.append(jnp.transpose(mark).astype(jnp.bfloat16))

    total[...] = jnp.zeros_like(total)

    def expand(i, _):
        load_wait(1, up_ref, up_vm, i)
        at = pl.ds(pl.multiple_of(i * span, span), span)
        base = (i * per).astype(jnp.float32).astype(jnp.bfloat16)
        m0, m1 = marks[0] - base, marks[1] - base
        nil = jnp.zeros_like(vectors[0])
        for j in range(per // 2):
            v = jnp.where(m0 == 2 * j, vectors[0], jnp.where(m1 == 2 * j, vectors[1], nil))
            mixed_rows[:, j * 2 * rank:(j + 1) * 2 * rank] = v
        total[...] += jnp.dot(mixed_rows[...], up_vm[at, :], preferred_element_type=jnp.float32)
        return 0

    lax.fori_loop(0, LOADS // 2, expand, 0)
    for q in range(Q):
        y_event(2, q)
    lax.fori_loop(LOADS // 2, LOADS, expand, 0)
    for q in range(Q):
        y_event(3, q)

    for q in range(Q):
        own[q].wait()
        for zz in [z] + far[1:]:
            for yy in (y, 1 - y):
                wait_in(q, dev(zz, yy, 1 - c))
        pltpu.make_async_copy(
            w_ref.at[pl.ds(q * kq, kq)], w_vm.at[pl.ds(q * kq, kq)], w_sem.at[q]).wait()
        part = total[...] + jnp.dot(
            gathered[q], w_vm[pl.ds(q * kq, kq), :], preferred_element_type=jnp.float32)
        if q < Q - 1:
            total[...] = part
        else:
            out_ref[...] = part.astype(out_ref.dtype)

    for cp, cond in sends:
        if cond is None:
            cp.wait_send()
        else:
            pl.when(cond)(cp.wait_send)


def by_kernel(rows, weight, down, up, picks, gates, index):
    stored, feat, rank = down.shape
    tokens = picks.shape[0]
    width = weight.shape[0]
    columns = weight.shape[1]
    span = stored // LOADS * rank
    any_ = pl.BlockSpec(memory_space=pl.ANY)
    vm = pl.BlockSpec(memory_space=pltpu.VMEM)
    dma = pltpu.SemaphoreType.DMA
    return pl.pallas_call(
        fused,
        out_shape=jax.ShapeDtypeStruct((tokens, columns), jnp.bfloat16),
        in_specs=[any_, any_, any_, any_, vm, vm, pl.BlockSpec(memory_space=pltpu.SMEM)],
        out_specs=vm,
        scratch_shapes=[
            pltpu.VMEM((Q, tokens, width // Q), jnp.bfloat16),
            pltpu.VMEM((tokens, feat), jnp.bfloat16),
            pltpu.VMEM((width, columns), jnp.bfloat16),
            pltpu.VMEM((stored * rank, feat), jnp.bfloat16),
            pltpu.VMEM((stored * rank, columns), jnp.bfloat16),
            pltpu.VMEM((tokens, span), jnp.bfloat16),
            pltpu.VMEM((N, 4 * rank // N, tokens // 2), jnp.bfloat16),
            pltpu.VMEM((N, 4 * rank // N, tokens // 2), jnp.bfloat16),
            pltpu.VMEM((N, 4 * rank // N, tokens // 2), jnp.bfloat16),
            pltpu.VMEM((tokens, columns), jnp.float32),
            dma((2, LOADS)), dma((Q,)), dma((Q + 1,)), dma((N,)), dma((N,)),
            dma((5, Q)), dma((4, Q)), dma((8, Q)), dma((Q, N)),
            dma((N,)), dma((N,)), dma((N,)), dma((N,)),
        ],
        compiler_params=pltpu.CompilerParams(
            collective_id=0, has_side_effects=True, vmem_limit_bytes=60 * 2**20),
        cost_estimate=pl.CostEstimate(
            flops=2 * tokens * columns * (width + 2 * stored * rank),
            bytes_accessed=2 * (weight.size + down.size + up.size), transcendentals=0),
    )(
        rows, weight, jnp.swapaxes(down, 1, 2).reshape(stored * rank, feat),
        up.reshape(stored * rank, columns), picks.T, gates.T, index,
    )


def routing(picks, gates, adapter_storage_index, storage_count, most):
    chosen = picks.reshape(-1)
    slot_of = jnp.take(adapter_storage_index, chosen)
    onehot = (slot_of[:, None] == jnp.arange(storage_count, dtype=jnp.int32)[None, :]).astype(
        jnp.int32
    )
    order_in = jnp.sum((jnp.cumsum(onehot, axis=0) - onehot) * onehot, axis=1)
    position = slot_of * most + order_in
    token_ids = jnp.arange(chosen.shape[0], dtype=jnp.int32) // 2
    token_of = jnp.zeros((storage_count * most,), jnp.int32).at[position].set(token_ids)
    token_gate_weight = (
        jnp.zeros((storage_count * most,), jnp.float32).at[position].set(gates.reshape(-1))
    )
    live = (
        jnp.zeros((storage_count * most,), jnp.float32)
        .at[position]
        .set(jnp.ones_like(gates.reshape(-1)))
    )
    return (token_of, token_gate_weight, live)


def by_collectives(rows, weight, down, up, picks, gates, index):
    storage_count = down.shape[0]
    most = max(2, 8 * picks.shape[0] // storage_count)
    columns = weight.shape[1]
    gathered = lax.all_gather(rows, "tensor", axis=0, tiled=True)
    base = jnp.dot(gathered, weight, preferred_element_type=jnp.float32)
    own_block = lax.dynamic_slice_in_dim(gathered, lax.axis_index("tensor") * columns, columns, 1)
    token_of, token_gate_weight, live = routing(picks, gates, index, storage_count, most)
    routed = (own_block[token_of] * live[:, None].astype(own_block.dtype)).reshape(
        storage_count, most, columns
    )
    partial = jnp.einsum("kit,ktn->kin", routed, down, preferred_element_type=jnp.float32)
    reduced = lax.psum(partial, "tensor").astype(jnp.bfloat16)
    expanded = jnp.einsum("hou,hut->hot", reduced, up, preferred_element_type=jnp.float32)
    expanded = expanded * token_gate_weight.reshape(storage_count, most)[:, :, None]
    total = base.at[token_of].add(expanded.reshape(storage_count * most, columns))
    return total.astype(jnp.bfloat16)


def solution(mesh):
    placed = (
        P(("groups", "tensor"), None),
        P(None, "tensor"),
        P(None, "tensor", None),
        P(None, None, "tensor"),
        P("groups", None),
        P("groups", None),
        P(),
    )
    body = by_kernel if mesh.shape["tensor"] == N else by_collectives
    return jax.shard_map(
        body, mesh=mesh, in_specs=placed, out_specs=P("groups", "tensor"), check_vma=False
    )
```
